32 devices in a mesh: tile: 8 (over y, x, core), mode: 4 (over z).
Axes of the slice: x: 2, y: 2, z: 4, core: 2. Of those that a mesh axis runs over, the one named last changes fastest.
Arguments:
- object_field: float32 [2, 4096, 384], P(None, 'tile'), may hold values from -4 to 4
- probe: float32 [4, 2, 256, 256], P('mode'), may hold values from -3 to 3
- intensities: bfloat16 [32, 256, 256], P('tile'), may hold values from 0.049804688 to 8
- scan_rows: int32 [32], P('tile'), may hold values from 0 to 511
- scan_cols: int32 [32], P('tile'), may hold values from 0 to 127
Outputs:
- updated_object: float32 [2, 4096, 384], P(None, 'tile')
- position_step: float32 [32, 2], P('tile')
The draws below stay inside these ranges and needn't reach their ends.
All inputs are finite; a program needn't handle non-finite values.
Results may differ from the reference program's by a relative error of at most 0.0003.
Values sent between devices are 32-bit elements; how exact they have to be, the bound alone decides.
A program may use at most 64 MiB of HBM per device.

```python
import math
import jax
import jax.numpy as jnp
from jax import lax

P_SIZE = 256
TR = 512
NC = 384
POS_DEV = 4
MODES = 4
NR = 4096
NPOS = 32


def place_ends(array, rng, smallest, largest):
    spot = [jax.random.randint(jax.random.fold_in(rng, axis), (), 0, length) for axis, length in enumerate(array.shape)]
    widest = array.shape.index(max(array.shape))
    next_to = spot[:widest] + [(spot[widest] + 1) % array.shape[widest]] + spot[widest + 1:]
    return array.at[tuple(spot)].set(smallest).at[tuple(next_to)].set(largest)


def steps_of(own_key, dims, pieces, least, high):
    def one(dim, shards_of):
        heights = jax.random.uniform(jax.random.fold_in(jax.random.fold_in(own_key, 6), dim), (shards_of,), jnp.float32, least / len(pieces), high / len(pieces))
        return jnp.repeat(jnp.exp(heights), dims[dim] // shards_of).reshape((-1,) + (1,) * (len(dims) - dim - 1))

    gain = one(*pieces[0])
    for cut in pieces[1:]:
        gain = gain * one(*cut)
    return gain


def normal_values(own_key, dims, scale, reach, shards=(), kind=jnp.bfloat16):
    entries = scale * jax.random.normal(own_key, dims, jnp.float32)
    if shards:
        entries = entries * steps_of(own_key, dims, shards, -0.22, 0.18)
    return jnp.clip(entries, -reach, reach).astype(kind)


def setup_inputs(seed: int = 0) -> dict:
    arg_keys = jax.random.split(jax.random.key(seed), 6)
    return {
        "object_field": normal_values(arg_keys[0], (2, NR, NC), 0.7, 4.0, ((1, 8),), jnp.float32),
        "probe": normal_values(arg_keys[1], (MODES, 2, P_SIZE, P_SIZE), 0.5, 3.0, ((0, 4),), jnp.float32),
        "intensities": jnp.clip(jnp.exp(math.log(8.0) - 5.0790877 * jax.random.uniform(arg_keys[2], (NPOS, P_SIZE, P_SIZE), jnp.float32) ** steps_of(arg_keys[2], (NPOS, P_SIZE, P_SIZE), ((0, 8),), -0.2, 0.2)), 0.049804688, 8.0).astype(jnp.bfloat16),
        "scan_rows": place_ends(jax.random.randint(arg_keys[3], (NPOS,), 0, TR), jax.random.fold_in(arg_keys[3], 1), 0, TR - 1).astype(jnp.int32),
        "scan_cols": place_ends(jax.random.randint(arg_keys[4], (NPOS,), 0, NC - P_SIZE), jax.random.fold_in(arg_keys[4], 1), 0, (NC - P_SIZE) - 1).astype(jnp.int32),
    }


damping = 0.5

def tables(side):
    numbers = jnp.arange(side, dtype=jnp.int32)
    product = numbers[:, None] * numbers[None, :] % side
    angles = product.astype(jnp.float32) * (2.0 * math.pi / side)
    return (jnp.cos(angles) / math.sqrt(side), jnp.sin(angles) / math.sqrt(side))

def left_mul(table, field):
    return jnp.einsum('jk,...kl->...jl', table, field, precision=lax.Precision.HIGHEST)

def right_mul(field, table):
    return jnp.einsum('...jk,kl->...jl', field, table, precision=lax.Precision.HIGHEST)

def transform(real_part, imag_part, cos_table, sin_table, factor):
    row_real = left_mul(cos_table, real_part) - factor * left_mul(sin_table, imag_part)
    row_imag = left_mul(cos_table, imag_part) + factor * left_mul(sin_table, real_part)
    out_real = right_mul(row_real, cos_table) - factor * right_mul(row_imag, sin_table)
    out_imag = right_mul(row_imag, cos_table) + factor * right_mul(row_real, sin_table)
    return (out_real, out_imag)

def reference(object_field, probe, intensities, scan_rows, scan_cols):
    side = P_SIZE
    cos_table, sin_table = tables(side)
    probe_real = probe[:, 0]
    probe_imag = probe[:, 1]
    illumination = lax.optimization_barrier(jnp.sum(probe_real * probe_real + probe_imag * probe_imag, axis=0))
    extended = jnp.concatenate([object_field, jnp.zeros((2, side, NC), jnp.float32)], axis=1)
    tile_of = (jnp.arange(NPOS, dtype=jnp.int32) // POS_DEV).astype(jnp.int32)
    global_rows = (tile_of * TR + scan_rows).astype(jnp.int32)

    def visit(frames, inputs):
        frame_grad, frame_light = frames
        row_start, col_start, measured = inputs
        zero = jnp.zeros((), jnp.int32)
        window = lax.dynamic_slice(extended, (zero, row_start, col_start), (2, side + 1, side + 1))
        patch_real = window[0, :side, :side]
        patch_imag = window[1, :side, :side]
        psi_real = probe_real * patch_real - probe_imag * patch_imag
        psi_imag = probe_real * patch_imag + probe_imag * patch_real
        far_real, far_imag = transform(psi_real, psi_imag, cos_table, sin_table, -1.0)
        intensity = lax.optimization_barrier(jnp.sum(far_real * far_real + far_imag * far_imag, axis=0))
        scaling = jnp.sqrt(measured.astype(jnp.float32)) / jnp.sqrt(jnp.maximum(intensity, 0.25)) - 1.0
        change_real, change_imag = transform(far_real * scaling, far_imag * scaling, cos_table, sin_table, 1.0)
        grad_real = lax.optimization_barrier(jnp.sum(probe_real * change_real + probe_imag * change_imag, axis=0))
        grad_imag = lax.optimization_barrier(jnp.sum(probe_real * change_imag - probe_imag * change_real, axis=0))
        steps = []
        for shifted in (window[:, 1:, :side], window[:, :side, 1:]):
            diff_real = shifted[0] - patch_real
            diff_imag = shifted[1] - patch_imag
            q_real = probe_real * diff_real - probe_imag * diff_imag
            q_imag = probe_real * diff_imag + probe_imag * diff_real
            numer = jnp.mean(q_real * change_real + q_imag * change_imag)
            denom = jnp.mean(q_real * q_real + q_imag * q_imag)
            steps.append(numer / (denom + 1e-06))
        grads = jnp.stack([grad_real, grad_imag])
        start = (zero, row_start, col_start)
        frame_grad = lax.dynamic_update_slice(frame_grad, lax.dynamic_slice(frame_grad, start, (2, side, side)) + grads, start)
        start_two = (row_start, col_start)
        frame_light = lax.dynamic_update_slice(frame_light, lax.dynamic_slice(frame_light, start_two, (side, side)) + illumination, start_two)
        return ((frame_grad, frame_light), jnp.stack(steps))
    initial = (jnp.zeros((2, NR + side, NC), jnp.float32), jnp.zeros((NR + side, NC), jnp.float32))
    (frame_grad, frame_light), position_step = lax.scan(visit, initial, (global_rows, scan_cols, intensities))
    updated_object = object_field + frame_grad[:, :NR] / (frame_light[:NR] + damping)[None]
    return (updated_object, position_step)
```

```python
import functools
import math

import jax
import jax.numpy as jnp
import numpy as np
from jax import lax
from jax.experimental import pallas as pl
from jax.experimental.pallas import tpu as pltpu
from jax.sharding import PartitionSpec as P

damping = 0.5
F32 = jnp.float32
BF16 = jnp.bfloat16


def from_behind(value, axis, steps):
    count = lax.axis_size(axis)
    first, last = (max(0, -steps), min(count, count - steps))
    return lax.ppermute(value, axis, [(source, source + steps) for source in range(first, last)])


def tables(side):
    half = side // 2
    k = np.arange(half)
    stack = []
    for odd in (0, 1):
        turn = (k[:, None] * (2 * k[None, :] + odd)) % side
        w = np.exp(-2j * math.pi * turn / side) / math.sqrt(side)
        real = np.block([[w.real, w.imag], [-w.imag, w.real]]).astype(np.float32)
        for table in (real, real.T):
            high = table.astype(jnp.bfloat16)
            low = (table - high.astype(np.float32)).astype(jnp.bfloat16)
            stack += [high, low]
    order = np.concatenate([np.arange(0, side, 2), np.arange(1, side, 2)])
    move = np.zeros((side, side), np.float32)
    move[np.arange(side), order] = 1.0
    stack += [move.astype(jnp.bfloat16), move.T.astype(jnp.bfloat16)]
    return np.stack(stack)


def split(x):
    high = x.astype(BF16)
    return high, (x - high.astype(F32)).astype(BF16)


def times(x, high, low):
    a, b = split(x)
    return jnp.dot(
        jnp.concatenate([a, b, a], axis=1),
        jnp.concatenate([high, high, low], axis=0),
        preferred_element_type=F32,
    )


def under(high, low, x):
    a, b = split(x)
    return jnp.dot(
        jnp.concatenate([high, high, low], axis=1),
        jnp.concatenate([a, b, a], axis=0),
        preferred_element_type=F32,
    )


def compute_kernel(
    rows_ref, cols_ref, prev_rows_ref, prev_cols_ref, ext, probe, measured, table,
    frame, light, stats, win, far, inten, pad, lightpad, lightbuf,
):
    positions = rows_ref.shape[0]
    modes, _, side, _ = probe.shape
    half = side // 2
    columns = ext.shape[2]
    tile_rows = light.shape[0]
    span = win.shape[1]

    def tab(odd, flip):
        i = 4 * odd + 2 * flip
        return table[i], table[i + 1]

    frame[...] = jnp.zeros_like(frame)
    lightbuf[...] = jnp.zeros_like(lightbuf)
    pad[...] = jnp.zeros_like(pad)
    lightpad[...] = jnp.zeros_like(lightpad)
    illumination = jnp.zeros((side, side), F32)
    for m in range(modes):
        illumination += probe[m, 0] * probe[m, 0] + probe[m, 1] * probe[m, 1]
    lightpad[:side, :side] = illumination

    def add_light(r, c, base):
        low = lax.rem(r, 8)
        at = pl.multiple_of(base + r - low, 8)
        x = pltpu.roll(pltpu.roll(lightpad[...], c, 1), low, 0)
        lightbuf[pl.ds(at, span), :] += x

    @pl.loop(0, positions)
    def _(p):
        add_light(rows_ref[p], cols_ref[p], tile_rows)
        add_light(prev_rows_ref[p], prev_cols_ref[p], 0)

    light[...] = lightbuf[tile_rows : 2 * tile_rows, :]

    @pl.loop(0, positions)
    def _(p):
        r = rows_ref[p]
        c = cols_ref[p]
        low = lax.rem(r, 8)
        base = pl.multiple_of(r - low, 8)
        for ch in range(2):
            x = ext[ch, pl.ds(base, span + 8), :]
            x = pltpu.roll(x, lax.rem(columns - c, columns), 1)
            x = pltpu.roll(x, lax.rem(span + 8 - low, span + 8), 0)
            win[ch] = x[:span]
        inten[...] = jnp.zeros_like(inten)

        @pl.loop(0, modes)
        def _(m):
            pr, pi = probe[m, 0], probe[m, 1]
            wr, wi = win[0, :side, :side], win[1, :side, :side]
            xr = pr * wr - pi * wi
            xi = pr * wi + pi * wr
            even = under(*tab(0, 1), jnp.concatenate([xr[:half] + xr[half:], xi[:half] + xi[half:]], 0))
            odd = under(*tab(1, 1), jnp.concatenate([xr[:half] - xr[half:], xi[:half] - xi[half:]], 0))
            sums, diffs = [], []
            for part in (even, odd):
                a, b = part[:, :half] + part[:, half:], part[:, :half] - part[:, half:]
                sums.append(jnp.concatenate([a[:half], a[half:]], 1))
                diffs.append(jnp.concatenate([b[:half], b[half:]], 1))
            fe = times(jnp.concatenate(sums, 0), *tab(0, 0))
            fo = times(jnp.concatenate(diffs, 0), *tab(1, 0))
            far[m, 0] = fe
            far[m, 1] = fo
            inten[:, :half] += fe[:, :half] * fe[:, :half] + fe[:, half:] * fe[:, half:]
            inten[:, half:] += fo[:, :half] * fo[:, :half] + fo[:, half:] * fo[:, half:]

        moved = jnp.dot(table[8], measured[p], preferred_element_type=F32).astype(BF16)
        moved = jnp.dot(moved, table[9], preferred_element_type=F32)
        inten[...] = jnp.sqrt(moved) / jnp.sqrt(jnp.maximum(inten[...], 0.25)) - 1.0
        pad[:, :side, :side] = jnp.zeros((2, side, side), F32)

        @pl.loop(0, modes)
        def _(m):
            se, so = inten[:, :half], inten[:, half:]
            u = times(far[m, 0] * jnp.concatenate([se, se], 1), *tab(0, 1))
            v = times(far[m, 1] * jnp.concatenate([so, so], 1), *tab(1, 1))
            a, b = u + v, u - v
            yr = jnp.concatenate([a[:, :half], b[:, :half]], 1)
            yi = jnp.concatenate([a[:, half:], b[:, half:]], 1)
            u = under(*tab(0, 0), jnp.concatenate([yr[:half], yi[:half]], 0))
            v = under(*tab(1, 0), jnp.concatenate([yr[half:], yi[half:]], 0))
            a, b = u + v, u - v
            cr = jnp.concatenate([a[:half], b[:half]], 0)
            ci = jnp.concatenate([a[half:], b[half:]], 0)
            pr, pi = probe[m, 0], probe[m, 1]
            pad[0, :side, :side] += pr * cr + pi * ci
            pad[1, :side, :side] += pr * ci - pi * cr

        gr, gi = pad[0, :side, :side], pad[1, :side, :side]
        wr, wi = win[0, :side, :side], win[1, :side, :side]
        shine = lightpad[:side, :side]
        for d in range(2):
            if d == 0:
                dr, di = win[0, 1 : side + 1, :side] - wr, win[1, 1 : side + 1, :side] - wi
            else:
                dr = pltpu.roll(win[0, :side, :], columns - 1, 1)[:, :side] - wr
                di = pltpu.roll(win[1, :side, :], columns - 1, 1)[:, :side] - wi
            stats[p, d : d + 1, :] = jnp.sum(dr * gr + di * gi, axis=0, keepdims=True)
            stats[p, d + 2 : d + 3, :] = jnp.sum((dr * dr + di * di) * shine, axis=0, keepdims=True)
        for ch in range(2):
            x = pltpu.roll(pltpu.roll(pad[ch], c, 1), low, 0)
            frame[ch, pl.ds(base, span), :] += x


def on_device(object_field, probe, intensities, scan_rows, scan_cols):
    tile_rows, columns = object_field.shape[1:]
    side = probe.shape[-1]
    positions = scan_rows.shape[0]
    modes = lax.axis_size("mode")
    span = side + 8
    following = from_behind(object_field[:, :side, :], "tile", -1)
    extended = jnp.concatenate(
        [object_field, following, jnp.zeros((2, 16, columns), F32)], axis=1
    )
    probes = lax.all_gather(probe, "mode", axis=0, tiled=True)
    prev_rows, prev_cols = from_behind((scan_rows, scan_cols), "tile", 1)
    smem = pl.BlockSpec(memory_space=pltpu.SMEM)
    vmem = pl.BlockSpec(memory_space=pltpu.VMEM)
    frame, light, stats = pl.pallas_call(
        compute_kernel,
        out_shape=(
            jax.ShapeDtypeStruct((2, tile_rows + side, columns), F32),
            jax.ShapeDtypeStruct((tile_rows, columns), F32),
            jax.ShapeDtypeStruct((positions, 4, side), F32),
        ),
        in_specs=[smem] * 4 + [vmem] * 4,
        out_specs=(vmem, vmem, vmem),
        scratch_shapes=[
            pltpu.VMEM((2, span, columns), F32),
            pltpu.VMEM((modes, 2, side, side), F32),
            pltpu.VMEM((side, side), F32),
            pltpu.VMEM((2, span, columns), F32),
            pltpu.VMEM((span, columns), F32),
            pltpu.VMEM((2 * tile_rows + side, columns), F32),
        ],
        compiler_params=pltpu.CompilerParams(vmem_limit_bytes=48 * 1024 * 1024),
    )(scan_rows, scan_cols, prev_rows, prev_cols, extended, probes, intensities, jnp.asarray(tables(side)))
    pixels = side * side
    terms = jnp.sum(stats, axis=2) / pixels / modes
    position_step = terms[:, :2] / (terms[:, 2:] + 1e-06)
    carried = from_behind(frame[:, tile_rows:], "tile", 1)
    own_grad = frame[:, :tile_rows].at[:, :side].add(carried)
    updated_object = object_field + own_grad / (light + damping)[None]
    return (updated_object, position_step)


def solution(mesh):
    in_specs = (
        P(None, "tile", None),
        P("mode", None, None, None),
        P("tile", None, None),
        P("tile"),
        P("tile"),
    )
    out_specs = (P(None, "tile", None), P("tile", None))
    return jax.shard_map(
        on_device, mesh=mesh, in_specs=in_specs, out_specs=out_specs, check_vma=False
    )
```

```python
import math

import jax
import jax.numpy as jnp
import numpy as np
from jax import lax
from jax.experimental import pallas as pl
from jax.experimental.pallas import tpu as pltpu
from jax.sharding import PartitionSpec as P

damping = 0.5
F32 = jnp.float32
BF16 = jnp.bfloat16
MESH = pl.DeviceIdType.MESH


def tables(side):
    half = side // 2
    k = np.arange(half)
    stack = []
    for odd in (0, 1):
        turn = (k[:, None] * (2 * k[None, :] + odd)) % side
        w = np.exp(-2j * math.pi * turn / side) / math.sqrt(side)
        real = np.block([[w.real, w.imag], [-w.imag, w.real]]).astype(np.float32)
        for table in (real, real.T):
            high = table.astype(jnp.bfloat16)
            low = (table - high.astype(np.float32)).astype(jnp.bfloat16)
            stack += [high, low]
    order = np.concatenate([np.arange(0, side, 2), np.arange(1, side, 2)])
    move = np.zeros((side, side), np.float32)
    move[np.arange(side), order] = 1.0
    stack += [move.astype(jnp.bfloat16), move.T.astype(jnp.bfloat16)]
    return np.stack(stack)


def split(x):
    high = x.astype(BF16)
    return high, (x - high.astype(F32)).astype(BF16)


def times(x, high, low):
    a, b = split(x)
    return jnp.dot(
        jnp.concatenate([a, b, a], axis=1),
        jnp.concatenate([high, high, low], axis=0),
        preferred_element_type=F32,
    )


def under(high, low, x):
    a, b = split(x)
    return jnp.dot(
        jnp.concatenate([high, high, low], axis=1),
        jnp.concatenate([a, b, a], axis=0),
        preferred_element_type=F32,
    )


def to(t, z):
    return dict(device_id=(t, z), device_id_type=MESH)


def gather_kernel(
    own, probe, scan_rows, scan_cols, following, probes, prev_rows, prev_cols,
    z_send, z_recv, y_send, y_recv, c_send, c_recv, h_send, h_recv, own_sem,
):
    tile, mode = lax.axis_index("tile"), lax.axis_index("mode")
    tiles, modes = lax.axis_size("tile"), lax.axis_size("mode")
    side = probe.shape[-1]
    half = side // 2
    core = lax.rem(tile, 2)
    sibling = tile + 1 - 2 * core
    upper = lax.rem(tile // 4, 2)
    across = tile + 4 - 8 * upper
    part = pl.ds(pl.multiple_of(upper * half, half), half)
    after, before = lax.rem(tile + 1, tiles), lax.rem(tile + tiles - 1, tiles)

    barrier = pltpu.get_barrier_semaphore()
    greeted = [(after, mode), (before, mode), (across, mode)]
    greeted += [(tile, lax.rem(mode + k, modes)) for k in range(1, modes)]
    for t, z in greeted:
        pl.semaphore_signal(barrier, inc=1, **to(t, z))
    pl.semaphore_wait(barrier, len(greeted))

    halo = pltpu.make_async_remote_copy(
        src_ref=own.at[:, :side, :], dst_ref=following,
        send_sem=h_send.at[0], recv_sem=h_recv.at[0], **to(before, mode))
    send_rows = pltpu.make_async_remote_copy(
        src_ref=scan_rows, dst_ref=prev_rows,
        send_sem=h_send.at[1], recv_sem=h_recv.at[1], **to(after, mode))
    send_cols = pltpu.make_async_remote_copy(
        src_ref=scan_cols, dst_ref=prev_cols,
        send_sem=h_send.at[2], recv_sem=h_recv.at[2], **to(after, mode))

    def over_modes(k):
        return pltpu.make_async_remote_copy(
            src_ref=probe.at[0, core, part, :], dst_ref=probes.at[mode, core, part, :],
            send_sem=z_send.at[k - 1], recv_sem=z_recv.at[k - 1], **to(tile, lax.rem(mode + k, modes)))

    def source(k):
        return lax.rem(mode + modes - k, modes)

    def over_y(k):
        at = probes.at[source(k), core, part, :]
        return pltpu.make_async_remote_copy(
            src_ref=at, dst_ref=at, send_sem=y_send.at[k - 1], recv_sem=y_recv.at[k - 1], **to(across, mode))

    def over_core(k):
        at = probes.at[source(k), core]
        return pltpu.make_async_remote_copy(
            src_ref=at, dst_ref=at, send_sem=c_send.at[k - 1], recv_sem=c_recv.at[k - 1], **to(sibling, mode))

    order = [k for k in (1, 3, 2) if k < modes] + list(range(4, modes))
    for k in order:
        over_modes(k).start()
    pl.when(tile > 0)(halo.start)
    send_rows.start()
    send_cols.start()
    keep = pltpu.make_async_copy(probe.at[0], probes.at[mode], own_sem.at[0])
    keep.start()
    for k in order:
        over_modes(k).wait_recv()
        over_y(k).start()
    for k in order:
        over_y(k).wait_recv()
        over_core(k).start()
    for k in order:
        over_core(k).wait_recv()
    keep.wait()
    pl.when(tile < tiles - 1)(halo.wait_recv)
    pl.when(tile > 0)(halo.wait_send)
    send_rows.wait()
    send_cols.wait()
    for k in order:
        over_modes(k).wait_send()
        over_y(k).wait_send()
        over_core(k).wait_send()


def compute_kernel(
    rows_ref, cols_ref, prev_rows_ref, prev_cols_ref, own, following, probes, measured, table,
    frame, light, steps, ext, win, far, inten, pad, lightpad, lightbuf, nums, dens, load_sem,
):
    tile, tiles = lax.axis_index("tile"), lax.axis_size("tile")
    positions = rows_ref.shape[0]
    modes, _, side, _ = probes.shape
    half = side // 2
    tile_rows, columns = own.shape[1:]
    span = win.shape[2]

    def tab(odd, flip):
        i = 4 * odd + 2 * flip
        return table[i], table[i + 1]

    load_own = pltpu.make_async_copy(own, ext.at[:, :tile_rows, :], load_sem.at[0])
    load_next = pltpu.make_async_copy(
        following, ext.at[:, tile_rows : tile_rows + side, :], load_sem.at[1])
    load_own.start()
    pl.when(tile < tiles - 1)(load_next.start)
    ext[:, tile_rows + side :, :] = jnp.zeros((2, ext.shape[1] - tile_rows - side, columns), F32)

    @pl.when(tile == tiles - 1)
    def _():
        ext[:, tile_rows : tile_rows + side, :] = jnp.zeros((2, side, columns), F32)

    for ref in (frame, lightbuf, pad, lightpad, inten):
        ref[...] = jnp.zeros_like(ref)
    illumination = jnp.zeros((side, side), F32)
    for m in range(modes):
        illumination += probes[m, 0] * probes[m, 0] + probes[m, 1] * probes[m, 1]
    lightpad[:side, :side] = illumination

    def add_light(r, c, base):
        low = lax.rem(r, 8)
        at = pl.multiple_of(base + r - low, 8)
        x = pltpu.roll(pltpu.roll(lightpad[...], c, 1), low, 0)
        lightbuf[pl.ds(at, span), :] += x

    @pl.loop(0, positions)
    def _(p):
        add_light(rows_ref[p], cols_ref[p], tile_rows)
        first = tile == 0
        add_light(jnp.where(first, 0, prev_rows_ref[p]), jnp.where(first, 0, prev_cols_ref[p]), 0)

    load_own.wait()
    pl.when(tile < tiles - 1)(load_next.wait)

    @pl.loop(0, positions)
    def _(p):
        r, c = rows_ref[p], cols_ref[p]
        low = lax.rem(r, 8)
        base = pl.multiple_of(r - low, 8)
        for ch in range(2):
            x = ext[ch, pl.ds(base, span + 8), :]
            x = pltpu.roll(x, lax.rem(columns - c, columns), 1)
            win[p, ch] = pltpu.roll(x, lax.rem(span + 8 - low, span + 8), 0)[:span]

    light[...] = lightbuf[tile_rows : 2 * tile_rows, :]

    def forward(p, m):
        pr, pi = probes[m, 0], probes[m, 1]
        wr, wi = win[p, 0, :side, :side], win[p, 1, :side, :side]
        xr = pr * wr - pi * wi
        xi = pr * wi + pi * wr
        even = under(*tab(0, 1), jnp.concatenate([xr[:half] + xr[half:], xi[:half] + xi[half:]], 0))
        odd = under(*tab(1, 1), jnp.concatenate([xr[:half] - xr[half:], xi[:half] - xi[half:]], 0))
        sums, diffs = [], []
        for x in (even, odd):
            a, b = x[:, :half] + x[:, half:], x[:, :half] - x[:, half:]
            sums.append(jnp.concatenate([a[:half], a[half:]], 1))
            diffs.append(jnp.concatenate([b[:half], b[half:]], 1))
        fe = times(jnp.concatenate(sums, 0), *tab(0, 0))
        fo = times(jnp.concatenate(diffs, 0), *tab(1, 0))
        far[p, m, 0] = fe
        far[p, m, 1] = fo
        inten[p, :, :half] += fe[:, :half] * fe[:, :half] + fe[:, half:] * fe[:, half:]
        inten[p, :, half:] += fo[:, :half] * fo[:, :half] + fo[:, half:] * fo[:, half:]

    pair = positions

    @pl.loop(0, modes)
    def _(m):
        @pl.loop(0, positions // pair)
        def _(q):
            for i in range(pair):
                forward(q * pair + i, m)

    @pl.loop(0, positions)
    def _(p):
        moved = jnp.dot(table[8], measured[p], preferred_element_type=F32).astype(BF16)
        moved = jnp.dot(moved, table[9], preferred_element_type=F32)
        inten[p] = moved * lax.rsqrt(moved * jnp.maximum(inten[p], 0.25)) - 1.0
        pad[:, :side, :side] = jnp.zeros((2, side, side), F32)

        def inverse(m):
            se, so = inten[p, :, :half], inten[p, :, half:]
            u = times(far[p, m, 0] * jnp.concatenate([se, se], 1), *tab(0, 1))
            v = times(far[p, m, 1] * jnp.concatenate([so, so], 1), *tab(1, 1))
            a, b = u + v, u - v
            yr = jnp.concatenate([a[:, :half], b[:, :half]], 1)
            yi = jnp.concatenate([a[:, half:], b[:, half:]], 1)
            u = under(*tab(0, 0), jnp.concatenate([yr[:half], yi[:half]], 0))
            v = under(*tab(1, 0), jnp.concatenate([yr[half:], yi[half:]], 0))
            a, b = u + v, u - v
            cr = jnp.concatenate([a[:half], b[:half]], 0)
            ci = jnp.concatenate([a[half:], b[half:]], 0)
            pr, pi = probes[m, 0], probes[m, 1]
            pad[0, :side, :side] += pr * cr + pi * ci
            pad[1, :side, :side] += pr * ci - pi * cr

        for m in range(modes):
            inverse(m)

        gr, gi = pad[0, :side, :side], pad[1, :side, :side]
        wr, wi = win[p, 0, :side, :side], win[p, 1, :side, :side]
        shine = lightpad[:side, :side]
        for d in range(2):
            if d == 0:
                dr, di = win[p, 0, 1 : side + 1, :side] - wr, win[p, 1, 1 : side + 1, :side] - wi
            else:
                dr = pltpu.roll(win[p, 0, :side, :], columns - 1, 1)[:, :side] - wr
                di = pltpu.roll(win[p, 1, :side, :], columns - 1, 1)[:, :side] - wi
            nums[d, pl.ds(p, 1), :] = jnp.sum(dr * gr + di * gi, axis=0, keepdims=True)
            dens[d, pl.ds(p, 1), :] = jnp.sum((dr * dr + di * di) * shine, axis=0, keepdims=True)
        r, c = rows_ref[p], cols_ref[p]
        low = lax.rem(r, 8)
        base = pl.multiple_of(r - low, 8)
        for ch in range(2):
            x = pltpu.roll(pltpu.roll(pad[ch], c, 1), low, 0)
            frame[ch, pl.ds(base, span), :] += x

    scale = 1.0 / (side * side * modes)
    for d in range(2):
        num = jnp.sum(nums[d], axis=1, keepdims=True) * scale
        den = jnp.sum(dens[d], axis=1, keepdims=True) * scale
        steps[:, d : d + 1] = num / (den + 1e-06)


def carry_kernel(frame, grad_in, h_send, h_recv):
    tile, mode = lax.axis_index("tile"), lax.axis_index("mode")
    tiles = lax.axis_size("tile")
    side = grad_in.shape[1]
    after, before = lax.rem(tile + 1, tiles), lax.rem(tile + tiles - 1, tiles)
    barrier = pltpu.get_barrier_semaphore()
    for t in (after, before):
        pl.semaphore_signal(barrier, inc=1, **to(t, mode))
    pl.semaphore_wait(barrier, 2)
    grad_out = pltpu.make_async_remote_copy(
        src_ref=frame.at[:, frame.shape[1] - side :, :], dst_ref=grad_in,
        send_sem=h_send.at[0], recv_sem=h_recv.at[0], **to(after, mode))
    pl.when(tile < tiles - 1)(grad_out.start)
    pl.when(tile > 0)(grad_out.wait_recv)
    pl.when(tile < tiles - 1)(grad_out.wait_send)


def on_device(object_field, probe, intensities, scan_rows, scan_cols):
    tile_rows, columns = object_field.shape[1:]
    side = probe.shape[-1]
    positions = scan_rows.shape[0]
    modes = lax.axis_size("mode")
    span = side + 8
    smem = pl.BlockSpec(memory_space=pltpu.SMEM)
    vmem = pl.BlockSpec(memory_space=pltpu.VMEM)
    anywhere = pl.BlockSpec(memory_space=pl.ANY)
    dma = pltpu.SemaphoreType.DMA
    shape = jax.ShapeDtypeStruct

    following, probes, prev_rows, prev_cols = pl.pallas_call(
        gather_kernel,
        out_shape=(
            shape((2, side, columns), F32),
            shape((modes, 2, side, side), F32),
            shape((positions,), jnp.int32),
            shape((positions,), jnp.int32),
        ),
        in_specs=[anywhere] * 4,
        out_specs=(anywhere,) * 4,
        scratch_shapes=[dma((modes - 1,))] * 6 + [dma((3,))] * 2 + [dma((1,))],
        compiler_params=pltpu.CompilerParams(collective_id=0, has_side_effects=True),
    )(object_field, probe, scan_rows, scan_cols)

    frame, light, position_step = pl.pallas_call(
        compute_kernel,
        out_shape=(
            shape((2, tile_rows + side, columns), F32),
            shape((tile_rows, columns), F32),
            shape((positions, 2), F32),
        ),
        in_specs=[smem] * 4 + [anywhere] * 2 + [vmem] * 3,
        out_specs=(vmem, vmem, vmem),
        scratch_shapes=[
            pltpu.VMEM((2, tile_rows + side + 16, columns), F32),
            pltpu.VMEM((positions, 2, span, columns), F32),
            pltpu.VMEM((positions, modes, 2, side, side), F32),
            pltpu.VMEM((positions, side, side), F32),
            pltpu.VMEM((2, span, columns), F32),
            pltpu.VMEM((span, columns), F32),
            pltpu.VMEM((2 * tile_rows + side, columns), F32),
            pltpu.VMEM((2, positions, side), F32),
            pltpu.VMEM((2, positions, side), F32),
            dma((2,)),
        ],
        compiler_params=pltpu.CompilerParams(vmem_limit_bytes=52 * 1024 * 1024),
    )(
        scan_rows, scan_cols, prev_rows, prev_cols,
        object_field, following, probes, intensities, jnp.asarray(tables(side)),
    )

    carried = pl.pallas_call(
        carry_kernel,
        out_shape=shape((2, side, columns), F32),
        in_specs=[anywhere],
        out_specs=anywhere,
        scratch_shapes=[dma((1,)), dma((1,))],
        compiler_params=pltpu.CompilerParams(collective_id=1, has_side_effects=True),
    )(frame)
    carried = jnp.where(lax.axis_index("tile") > 0, carried, 0.0)

    grad = frame[:, :tile_rows] + jnp.pad(carried, ((0, 0), (0, tile_rows - side), (0, 0)))
    updated_object = object_field + grad / (light + damping)[None]
    return (updated_object, position_step)


def solution(mesh):
    in_specs = (
        P(None, "tile", None),
        P("mode", None, None, None),
        P("tile", None, None),
        P("tile"),
        P("tile"),
    )
    out_specs = (P(None, "tile", None), P("tile", None))
    return jax.shard_map(
        on_device, mesh=mesh, in_specs=in_specs, out_specs=out_specs, check_vma=False
    )
```

```python
import math

import jax
import jax.numpy as jnp
import numpy as np
from jax import lax
from jax.experimental import pallas as pl
from jax.experimental.pallas import tpu as pltpu
from jax.sharding import PartitionSpec as P

damping = 0.5
F32 = jnp.float32
BF16 = jnp.bfloat16
MESH = pl.DeviceIdType.MESH


def tables(side):
    half = side // 2
    k = np.arange(half)
    stack = []
    for odd in (0, 1):
        turn = (k[:, None] * (2 * k[None, :] + odd)) % side
        w = np.exp(-2j * math.pi * turn / side) / math.sqrt(side)
        real = np.block([[w.real, w.imag], [-w.imag, w.real]]).astype(np.float32)
        for table in (real, real.T):
            high = table.astype(jnp.bfloat16)
            low = (table - high.astype(np.float32)).astype(jnp.bfloat16)
            stack += [high, low]
    order = np.concatenate([np.arange(0, side, 2), np.arange(1, side, 2)])
    move = np.zeros((side, side), np.float32)
    move[np.arange(side), order] = 1.0
    stack += [move.astype(jnp.bfloat16), move.T.astype(jnp.bfloat16)]
    return np.stack(stack)


def split(x):
    high = x.astype(BF16)
    return high, (x - high.astype(F32)).astype(BF16)


def times(x, high, low):
    a, b = split(x)
    return jnp.dot(
        jnp.concatenate([a, b, a], axis=1),
        jnp.concatenate([high, high, low], axis=0),
        preferred_element_type=F32,
    )


def under(high, low, x):
    a, b = split(x)
    return jnp.dot(
        jnp.concatenate([high, high, low], axis=1),
        jnp.concatenate([a, b, a], axis=0),
        preferred_element_type=F32,
    )


def to(t, z):
    return dict(device_id=(t, z), device_id_type=MESH)


def gather_kernel(
    own, probe, scans, following, probes, prev_scans,
    z_send, z_recv, y_send, y_recv, c_send, c_recv, h_send, h_recv, own_sem,
):
    tile, mode = lax.axis_index("tile"), lax.axis_index("mode")
    tiles, modes = lax.axis_size("tile"), lax.axis_size("mode")
    side = probe.shape[-1]
    half = side // 2
    core = lax.rem(tile, 2)
    sibling = tile + 1 - 2 * core
    upper = lax.rem(tile // 4, 2)
    across = tile + 4 - 8 * upper
    part = pl.ds(pl.multiple_of(upper * half, half), half)
    after, before = lax.rem(tile + 1, tiles), lax.rem(tile + tiles - 1, tiles)

    barrier = pltpu.get_barrier_semaphore()
    greeted = [(after, mode), (before, mode), (across, mode)]
    greeted += [(tile, lax.rem(mode + k, modes)) for k in range(1, modes)]
    for t, z in greeted:
        pl.semaphore_signal(barrier, inc=1, **to(t, z))
    pl.semaphore_wait(barrier, len(greeted))

    halo = pltpu.make_async_remote_copy(
        src_ref=own.at[:, :side, :], dst_ref=following,
        send_sem=h_send.at[0], recv_sem=h_recv.at[0], **to(before, mode))
    send_scans = pltpu.make_async_remote_copy(
        src_ref=scans, dst_ref=prev_scans,
        send_sem=h_send.at[1], recv_sem=h_recv.at[1], **to(after, mode))

    def over_modes(k):
        return pltpu.make_async_remote_copy(
            src_ref=probe.at[0, core, part, :], dst_ref=probes.at[mode, core, part, :],
            send_sem=z_send.at[k - 1], recv_sem=z_recv.at[k - 1], **to(tile, lax.rem(mode + k, modes)))

    def source(k):
        return lax.rem(mode + modes - k, modes)

    def over_y(k):
        at = probes.at[source(k), core, part, :]
        return pltpu.make_async_remote_copy(
            src_ref=at, dst_ref=at, send_sem=y_send.at[k - 1], recv_sem=y_recv.at[k - 1], **to(across, mode))

    def over_core(k):
        at = probes.at[source(k), core]
        return pltpu.make_async_remote_copy(
            src_ref=at, dst_ref=at, send_sem=c_send.at[k - 1], recv_sem=c_recv.at[k - 1], **to(sibling, mode))

    order = [k for k in (1, 3, 2) if k < modes] + list(range(4, modes))
    for k in order:
        over_modes(k).start()
    pl.when(tile > 0)(halo.start)
    send_scans.start()
    keep = pltpu.make_async_copy(probe.at[0], probes.at[mode], own_sem.at[0])
    keep.start()
    for k in order:
        over_modes(k).wait_recv()
        over_y(k).start()
    for k in order:
        over_y(k).wait_recv()
        over_core(k).start()
    for k in order:
        over_core(k).wait_recv()
    keep.wait()
    pl.when(tile < tiles - 1)(halo.wait_recv)
    pl.when(tile > 0)(halo.wait_send)
    send_scans.wait()
    for k in order:
        over_modes(k).wait_send()
        over_y(k).wait_send()
        over_core(k).wait_send()


def compute_kernel(
    rows_ref, cols_ref, prev_ref, own, following, probes, measured, table,
    frame, light, steps, ext, win, far, inten, pad, lightpad, lightbuf, nums, dens, load_sem,
):
    tile, tiles = lax.axis_index("tile"), lax.axis_size("tile")
    positions = rows_ref.shape[0]
    modes, _, side, _ = probes.shape
    half = side // 2
    tile_rows, columns = own.shape[1:]
    span = win.shape[2]

    def tab(odd, flip):
        i = 4 * odd + 2 * flip
        return table[i], table[i + 1]

    load_own = pltpu.make_async_copy(own, ext.at[:, :tile_rows, :], load_sem.at[0])
    load_next = pltpu.make_async_copy(
        following, ext.at[:, tile_rows : tile_rows + side, :], load_sem.at[1])
    load_own.start()
    pl.when(tile < tiles - 1)(load_next.start)
    ext[:, tile_rows + side :, :] = jnp.zeros((2, ext.shape[1] - tile_rows - side, columns), F32)

    @pl.when(tile == tiles - 1)
    def _():
        ext[:, tile_rows : tile_rows + side, :] = jnp.zeros((2, side, columns), F32)

    for ref in (frame, lightbuf, pad, lightpad, inten):
        ref[...] = jnp.zeros_like(ref)
    illumination = jnp.zeros((side, side), F32)
    for m in range(modes):
        illumination += probes[m, 0] * probes[m, 0] + probes[m, 1] * probes[m, 1]
    lightpad[:side, :side] = illumination

    def add_light(r, c, base):
        low = lax.rem(r, 8)
        at = pl.multiple_of(base + r - low, 8)
        x = pltpu.roll(pltpu.roll(lightpad[...], c, 1), low, 0)
        lightbuf[pl.ds(at, span), :] += x

    @pl.loop(0, positions)
    def _(p):
        add_light(rows_ref[p], cols_ref[p], tile_rows)
        first = tile == 0
        add_light(jnp.where(first, 0, prev_ref[p]), jnp.where(first, 0, prev_ref[positions + p]), 0)

    load_own.wait()
    pl.when(tile < tiles - 1)(load_next.wait)

    @pl.loop(0, positions)
    def _(p):
        r, c = rows_ref[p], cols_ref[p]
        low = lax.rem(r, 8)
        base = pl.multiple_of(r - low, 8)
        for ch in range(2):
            x = ext[ch, pl.ds(base, span + 8), :]
            x = pltpu.roll(x, lax.rem(columns - c, columns), 1)
            win[p, ch] = pltpu.roll(x, lax.rem(span + 8 - low, span + 8), 0)[:span]

    light[...] = lightbuf[tile_rows : 2 * tile_rows, :]

    def forward(p, m):
        pr, pi = probes[m, 0], probes[m, 1]
        wr, wi = win[p, 0, :side, :side], win[p, 1, :side, :side]
        xr = pr * wr - pi * wi
        xi = pr * wi + pi * wr
        even = under(*tab(0, 1), jnp.concatenate([xr[:half] + xr[half:], xi[:half] + xi[half:]], 0))
        odd = under(*tab(1, 1), jnp.concatenate([xr[:half] - xr[half:], xi[:half] - xi[half:]], 0))
        sums, diffs = [], []
        for x in (even, odd):
            a, b = x[:, :half] + x[:, half:], x[:, :half] - x[:, half:]
            sums.append(jnp.concatenate([a[:half], a[half:]], 1))
            diffs.append(jnp.concatenate([b[:half], b[half:]], 1))
        fe = times(jnp.concatenate(sums, 0), *tab(0, 0))
        fo = times(jnp.concatenate(diffs, 0), *tab(1, 0))
        far[p, m, 0] = fe
        far[p, m, 1] = fo
        inten[p, :, :half] += fe[:, :half] * fe[:, :half] + fe[:, half:] * fe[:, half:]
        inten[p, :, half:] += fo[:, :half] * fo[:, :half] + fo[:, half:] * fo[:, half:]

    pair = positions

    @pl.loop(0, modes)
    def _(m):
        @pl.loop(0, positions // pair)
        def _(q):
            for i in range(pair):
                forward(q * pair + i, m)

    @pl.loop(0, positions)
    def _(p):
        moved = jnp.dot(table[8], measured[p], preferred_element_type=F32).astype(BF16)
        moved = jnp.dot(moved, table[9], preferred_element_type=F32)
        inten[p] = moved * lax.rsqrt(moved * jnp.maximum(inten[p], 0.25)) - 1.0
        pad[:, :side, :side] = jnp.zeros((2, side, side), F32)

        def inverse(m):
            se, so = inten[p, :, :half], inten[p, :, half:]
            u = times(far[p, m, 0] * jnp.concatenate([se, se], 1), *tab(0, 1))
            v = times(far[p, m, 1] * jnp.concatenate([so, so], 1), *tab(1, 1))
            a, b = u + v, u - v
            yr = jnp.concatenate([a[:, :half], b[:, :half]], 1)
            yi = jnp.concatenate([a[:, half:], b[:, half:]], 1)
            u = under(*tab(0, 0), jnp.concatenate([yr[:half], yi[:half]], 0))
            v = under(*tab(1, 0), jnp.concatenate([yr[half:], yi[half:]], 0))
            a, b = u + v, u - v
            cr = jnp.concatenate([a[:half], b[:half]], 0)
            ci = jnp.concatenate([a[half:], b[half:]], 0)
            pr, pi = probes[m, 0], probes[m, 1]
            pad[0, :side, :side] += pr * cr + pi * ci
            pad[1, :side, :side] += pr * ci - pi * cr

        for m in range(modes):
            inverse(m)

        gr, gi = pad[0, :side, :side], pad[1, :side, :side]
        wr, wi = win[p, 0, :side, :side], win[p, 1, :side, :side]
        shine = lightpad[:side, :side]
        for d in range(2):
            if d == 0:
                dr, di = win[p, 0, 1 : side + 1, :side] - wr, win[p, 1, 1 : side + 1, :side] - wi
            else:
                dr = pltpu.roll(win[p, 0, :side, :], columns - 1, 1)[:, :side] - wr
                di = pltpu.roll(win[p, 1, :side, :], columns - 1, 1)[:, :side] - wi
            nums[d, pl.ds(p, 1), :] = jnp.sum(dr * gr + di * gi, axis=0, keepdims=True)
            dens[d, pl.ds(p, 1), :] = jnp.sum((dr * dr + di * di) * shine, axis=0, keepdims=True)
        r, c = rows_ref[p], cols_ref[p]
        low = lax.rem(r, 8)
        base = pl.multiple_of(r - low, 8)
        for ch in range(2):
            x = pltpu.roll(pltpu.roll(pad[ch], c, 1), low, 0)
            frame[ch, pl.ds(base, span), :] += x

    scale = 1.0 / (side * side * modes)
    for d in range(2):
        num = jnp.sum(nums[d], axis=1, keepdims=True) * scale
        den = jnp.sum(dens[d], axis=1, keepdims=True) * scale
        steps[:, d : d + 1] = num / (den + 1e-06)


def carry_kernel(frame, zeros, grad_in, h_send, h_recv, zero_sem):
    tile, mode = lax.axis_index("tile"), lax.axis_index("mode")
    tiles = lax.axis_size("tile")
    side = grad_in.shape[1]
    after, before = lax.rem(tile + 1, tiles), lax.rem(tile + tiles - 1, tiles)
    barrier = pltpu.get_barrier_semaphore()
    for t in (after, before):
        pl.semaphore_signal(barrier, inc=1, **to(t, mode))
    pl.semaphore_wait(barrier, 2)
    grad_out = pltpu.make_async_remote_copy(
        src_ref=frame.at[:, frame.shape[1] - side :, :], dst_ref=grad_in,
        send_sem=h_send.at[0], recv_sem=h_recv.at[0], **to(after, mode))
    clear = pltpu.make_async_copy(zeros, grad_in, zero_sem.at[0])
    pl.when(tile < tiles - 1)(grad_out.start)
    pl.when(tile == 0)(clear.start)
    pl.when(tile == 0)(clear.wait)
    pl.when(tile > 0)(grad_out.wait_recv)
    pl.when(tile < tiles - 1)(grad_out.wait_send)


def on_device(object_field, probe, intensities, scan_rows, scan_cols):
    tile_rows, columns = object_field.shape[1:]
    side = probe.shape[-1]
    positions = scan_rows.shape[0]
    modes = lax.axis_size("mode")
    span = side + 8
    smem = pl.BlockSpec(memory_space=pltpu.SMEM)
    vmem = pl.BlockSpec(memory_space=pltpu.VMEM)
    anywhere = pl.BlockSpec(memory_space=pl.ANY)
    dma = pltpu.SemaphoreType.DMA
    shape = jax.ShapeDtypeStruct

    following, probes, prev_scans = pl.pallas_call(
        gather_kernel,
        out_shape=(
            shape((2, side, columns), F32),
            shape((modes, 2, side, side), F32),
            shape((2 * positions,), jnp.int32),
        ),
        in_specs=[anywhere] * 3,
        out_specs=(anywhere,) * 3,
        scratch_shapes=[dma((modes - 1,))] * 6 + [dma((3,))] * 2 + [dma((1,))],
        compiler_params=pltpu.CompilerParams(collective_id=0, has_side_effects=True),
    )(object_field, probe, jnp.concatenate([scan_rows, scan_cols]))

    frame, light, position_step = pl.pallas_call(
        compute_kernel,
        out_shape=(
            shape((2, tile_rows + side, columns), F32),
            shape((tile_rows, columns), F32),
            shape((positions, 2), F32),
        ),
        in_specs=[smem] * 3 + [anywhere] * 2 + [vmem] * 3,
        out_specs=(vmem, vmem, vmem),
        scratch_shapes=[
            pltpu.VMEM((2, tile_rows + side + 16, columns), F32),
            pltpu.VMEM((positions, 2, span, columns), F32),
            pltpu.VMEM((positions, modes, 2, side, side), F32),
            pltpu.VMEM((positions, side, side), F32),
            pltpu.VMEM((2, span, columns), F32),
            pltpu.VMEM((span, columns), F32),
            pltpu.VMEM((2 * tile_rows + side, columns), F32),
            pltpu.VMEM((2, positions, side), F32),
            pltpu.VMEM((2, positions, side), F32),
            dma((2,)),
        ],
        compiler_params=pltpu.CompilerParams(vmem_limit_bytes=52 * 1024 * 1024),
    )(
        scan_rows, scan_cols, prev_scans,
        object_field, following, probes, intensities, jnp.asarray(tables(side)),
    )

    carried = pl.pallas_call(
        carry_kernel,
        out_shape=shape((2, side, columns), F32),
        in_specs=[anywhere] * 2,
        out_specs=anywhere,
        scratch_shapes=[dma((1,))] * 3,
        compiler_params=pltpu.CompilerParams(collective_id=1, has_side_effects=True),
    )(frame, jnp.zeros((2, side, columns), F32))

    grad = frame[:, :tile_rows] + jnp.pad(carried, ((0, 0), (0, tile_rows - side), (0, 0)))
    updated_object = object_field + grad / (light + damping)[None]
    return (updated_object, position_step)


def solution(mesh):
    in_specs = (
        P(None, "tile", None),
        P("mode", None, None, None),
        P("tile", None, None),
        P("tile"),
        P("tile"),
    )
    out_specs = (P(None, "tile", None), P("tile", None))
    return jax.shard_map(
        on_device, mesh=mesh, in_specs=in_specs, out_specs=out_specs, check_vma=False
    )
```
